32 devices in a mesh: group: 2 (over x), attn: 8 (over z, y), expert: 2 (over core).
Axes of the slice: x: 2, y: 2, z: 4, core: 2. Of those that a mesh axis runs over, the one named last changes fastest.
Arguments:
- queries: bfloat16 [384, 48, 128], P(('group', 'attn'), 'expert'), parts along dimension 0, may hold values from -9 to 9
- keys: bfloat16 [384, 40, 8, 128], P(('group', 'attn'), None, 'expert'), parts along dimension 0, may hold values from -9 to 9
- values: bfloat16 [384, 40, 8, 128], P(('group', 'attn'), None, 'expert'), parts along dimension 0, may hold values from -12 to 12
- lengths: int32 [384], P(('group', 'attn')), parts along dimension 0, may hold values from 10 to 40, as said below
- out_proj: bfloat16 [6144, 3072], P('expert', 'attn'), may hold values from -0.078125 to 0.078125
- residual: bfloat16 [384, 3072], P('group', 'attn'), parts along dimension 0, may hold values from -45 to 45
- norm_gain: float32 [3072], replicated, may hold values from 0.25 to 1.75
- expert_ids: int32 [384, 2], P('group'), parts along dimension 0, may hold values from 0 to 3, as said below
- expert_slots: int32 [384, 2], P('group'), parts along dimension 0, may hold values from 0 to 143, as said below
- route_weights: float32 [384, 2], P('group'), parts along dimension 0, may hold values from 0.1 to 0.9
- w_gate: bfloat16 [4, 3072, 8192], P('expert', None, 'attn'), may hold values from -0.109375 to 0.109375
- w_up: bfloat16 [4, 3072, 8192], P('expert', None, 'attn'), may hold values from -0.109375 to 0.109375
- w_down: bfloat16 [4, 8192, 3072], P('expert', 'attn'), may hold values from -0.0625 to 0.0625
Outputs:
- hidden: bfloat16 [384, 3072], P('group', 'attn'), parts along dimension 0
- expert_out: bfloat16 [384, 3072], P('group', 'attn'), parts along dimension 0
The draws below stay inside these ranges and needn't reach their ends.
There are 2 independent parts, one for each index of `group`. The reference program is written for one: setup_inputs(seed, part) draws one part's arguments, and reference() takes and returns one part's arrays. A program takes and returns all parts, laid end to end along the dimension named above; an argument that names none is the same for every part. Nothing has to cross between parts.
Inputs may be any that keep to these rules, and one draw needn't show every extreme that they name: Each sequence's cache is live in its first lengths positions; one sequence is 40 long. `expert_ids`: the two experts of a token differ; one expert, drawn from the seed, is chosen by exactly 144 tokens, and the other three share the remaining choices nearly evenly. `expert_slots`: a choice's slot is its rank, counting tokens in order and a token's first choice before its second, among the choices of the same expert.
All inputs are finite; a program needn't handle non-finite values.
Results may differ from the reference program's by a relative error of at most 0.02.
Values may be sent and summed in bfloat16 or wider, within the bound.
A program may use at most 128 MiB of HBM per device.

```python
import math
import jax
import jax.numpy as jnp
from jax import lax

D = 3072
HEADS = 48
KV_HEADS = 8
HEAD_DIM = 128
EXPERTS = 4
FF = 8192
LMAX = 40
SEQ = 192
CAP = 144
N_ATTN = 8
N_EXPERT = 2


def route_table(key):
    ranks = jax.random.permutation(jax.random.fold_in(key, 11), SEQ).astype(jnp.int32)
    hot_expert = jax.random.randint(jax.random.fold_in(key, 12), (), 0, EXPERTS)
    cycle_pos = ranks % 3 + 1
    is_hot = ranks < CAP
    second_hot = (hot_expert + cycle_pos) % EXPERTS
    first_cold = (hot_expert + cycle_pos % 3 + 1) % EXPERTS
    second_cold = (hot_expert + (cycle_pos + 1) % 3 + 1) % EXPERTS
    first_pick = jnp.where(is_hot, hot_expert, first_cold)
    second_pick = jnp.where(is_hot, second_hot, second_cold)
    flips = jax.random.randint(jax.random.fold_in(key, 13), (SEQ,), 0, 2)
    left_pick = jnp.where(flips == 1, second_pick, first_pick)
    right_pick = jnp.where(flips == 1, first_pick, second_pick)
    chosen_ids = jnp.stack([left_pick, right_pick], axis=-1).astype(jnp.int32)
    onehot = (chosen_ids.reshape(-1)[:, None] == jnp.arange(EXPERTS)[None, :]).astype(jnp.int32)
    before = jnp.cumsum(onehot, axis=0) - onehot
    slot_rank = jnp.sum(before * onehot, axis=1).reshape(SEQ, 2).astype(jnp.int32)
    return (chosen_ids, slot_rank)


def draw_queries(key, part):
    key = jax.random.fold_in(key, 1)
    base_draw = jnp.clip(jax.random.normal(key, (SEQ, HEADS, HEAD_DIM)), -6.0, 6.0)
    return base_draw.astype(jnp.bfloat16)


def draw_keys(key, part):
    key = jax.random.fold_in(key, 2)
    base_draw = jnp.clip(jax.random.normal(key, (SEQ, LMAX, KV_HEADS, HEAD_DIM)), -6.0, 6.0)
    return base_draw.astype(jnp.bfloat16)


def draw_lengths(key, part):
    key = jax.random.fold_in(key, 5)
    drawn = jax.random.randint(jax.random.fold_in(key, 1), (SEQ,), LMAX // 4, LMAX + 1)
    longest = jax.random.randint(jax.random.fold_in(key, 2), (), 0, SEQ)
    return drawn.at[longest].set(LMAX).astype(jnp.int32)


def draw_residual(key, part):
    key = jax.random.fold_in(key, 3)
    row_scale = 0.3 * jnp.exp(jax.random.uniform(jax.random.fold_in(key, 1), (SEQ, 1)) * math.log(10.0))
    col_rise = jnp.exp(jnp.arange(D)[None, :] / D * math.log(3.0))
    col_scale = 0.3 * col_rise * jnp.exp(jax.random.uniform(jax.random.fold_in(key, 2), (1, D)) * math.log(10.0 / 3.0))
    base_draw = jnp.clip(jax.random.normal(jax.random.fold_in(key, 3), (SEQ, D)), -5.0, 5.0)
    return (base_draw * row_scale * col_scale).astype(jnp.bfloat16)


def draw_expert_ids(key, part):
    chosen_ids, slot_rank = route_table(key)
    return chosen_ids


def draw_expert_slots(key, part):
    chosen_ids, slot_rank = route_table(key)
    return slot_rank


def levels(key, shape, pieces, low, high):
    gain = 1.0
    for dim, shards_of in pieces:
        draws = jax.random.uniform(jax.random.fold_in(jax.random.fold_in(key, 6), dim), (shards_of,), jnp.float32, low / len(pieces), high / len(pieces))
        gain = gain * jnp.repeat(jnp.exp(draws), shape[dim] // shards_of).reshape((-1,) + (1,) * (len(shape) - 1 - dim))
    return gain


def centred(stream_key, shape, scale, most, cuts=(), held_as=jnp.bfloat16):
    level = levels(stream_key, shape, cuts, -0.22, 0.18) if cuts else 1.0
    values = jax.random.normal(stream_key, shape, jnp.float32) * scale * level
    return jnp.minimum(jnp.maximum(values, -most), most).astype(held_as)


def setup_inputs(seed: int = 0, part: int = 0) -> dict:
    streams_of = jax.random.split(jax.random.key(seed), 14)
    own_keys = jax.random.split(jax.random.fold_in(streams_of[13], part), 14)
    queries = draw_queries(jax.random.fold_in(jax.random.fold_in(streams_of[13], part), 71), part)
    keys = draw_keys(jax.random.fold_in(jax.random.fold_in(streams_of[13], part), 71), part)
    values = centred(own_keys[2], (SEQ, LMAX, KV_HEADS, HEAD_DIM), 2.0, 12.0, ((0, 8), (2, 2)))
    lengths = draw_lengths(jax.random.fold_in(jax.random.fold_in(streams_of[13], part), 71), part)
    out_proj = centred(streams_of[4], (HEADS * HEAD_DIM, D), (HEADS * HEAD_DIM) ** -0.5, 0.078125, ((0, 2), (1, 8)))
    residual = draw_residual(jax.random.fold_in(jax.random.fold_in(streams_of[13], part), 71), part)
    norm_gain = jnp.clip(1.0 + 0.15 * jax.random.normal(streams_of[6], (D,), jnp.float32), 0.25, 1.75)
    expert_ids = draw_expert_ids(jax.random.fold_in(jax.random.fold_in(streams_of[13], part), 71), part)
    expert_slots = draw_expert_slots(jax.random.fold_in(jax.random.fold_in(streams_of[13], part), 71), part)
    route_weights = jnp.clip(jax.random.uniform(own_keys[9], (SEQ, 2), jnp.float32, 0.1, 0.9), 0.1, 0.9)
    w_gate = centred(streams_of[10], (EXPERTS, D, FF), D ** -0.5, 0.109375, ((0, 2), (2, 8)))
    w_up = centred(streams_of[11], (EXPERTS, D, FF), D ** -0.5, 0.109375, ((0, 2), (2, 8)))
    w_down = centred(streams_of[12], (EXPERTS, FF, D), FF ** -0.5, 0.0625, ((0, 2), (1, 8)))
    return dict(queries=queries, keys=keys, values=values, lengths=lengths, out_proj=out_proj, residual=residual, norm_gain=norm_gain, expert_ids=expert_ids, expert_slots=expert_slots, route_weights=route_weights, w_gate=w_gate, w_up=w_up, w_down=w_down)


norm_eps = 1e-05

def expert_active(operands):
    rows_in, gate_w, up_w = operands
    gate_act = jnp.dot(rows_in, gate_w, preferred_element_type=jnp.float32)
    up_act = jnp.dot(rows_in, up_w, preferred_element_type=jnp.float32)
    return (jax.nn.silu(gate_act) * up_act).astype(jnp.bfloat16)

def reference(queries, keys, values, lengths, out_proj, residual, norm_gain, expert_ids, expert_slots, route_weights, w_gate, w_up, w_down):
    seq_count = queries.shape[0]
    cache_len = keys.shape[1]
    groups = HEADS // KV_HEADS
    query_groups = queries.astype(jnp.float32).reshape(seq_count, KV_HEADS, groups, HEAD_DIM)
    scores = jnp.einsum('skgd,sjkd->skgj', query_groups, keys.astype(jnp.float32)) / math.sqrt(HEAD_DIM)
    visible = lax.broadcasted_iota(jnp.int32, (seq_count, cache_len), 1) < lengths[:, None]
    scores = jnp.where(visible[:, None, None, :], scores, -jnp.inf)
    row_peak = lax.optimization_barrier(jnp.max(scores, axis=-1, keepdims=True))
    expo = jnp.exp(scores - row_peak)
    attn_probs = (expo / lax.optimization_barrier(jnp.sum(expo, axis=-1, keepdims=True))).astype(jnp.bfloat16)
    head_out = jnp.einsum('skgj,sjkd->skgd', attn_probs.astype(jnp.float32), values.astype(jnp.float32))
    head_out = head_out.astype(jnp.bfloat16).reshape(seq_count, HEADS * HEAD_DIM)
    mixed = jnp.dot(head_out, out_proj, preferred_element_type=jnp.float32)
    hidden = (residual.astype(jnp.float32) + mixed).astype(jnp.bfloat16)
    hidden_f = hidden.astype(jnp.float32)
    mean_sq = lax.optimization_barrier(jnp.mean(hidden_f * hidden_f, axis=1, keepdims=True))
    normed = (hidden_f * lax.rsqrt(mean_sq + norm_eps) * norm_gain[None, :]).astype(jnp.bfloat16)
    capacity = 3 * seq_count // 4
    flat_slot = (expert_ids * capacity + expert_slots).astype(jnp.int32)
    token_index = lax.broadcasted_iota(jnp.int32, (seq_count, 2), 0)
    slot_token = jnp.full((EXPERTS * capacity,), -1, jnp.int32).at[flat_slot.reshape(-1)].set(token_index.reshape(-1))
    filled = slot_token >= 0
    packed = jnp.where(filled[:, None], normed[jnp.maximum(slot_token, 0)], jnp.zeros((), jnp.bfloat16))
    packed = packed.astype(jnp.bfloat16).reshape(EXPERTS, capacity, D)
    active_all = lax.map(expert_active, (packed, w_gate, w_up))
    shard_width = FF // N_ATTN
    per_half = EXPERTS // N_EXPERT
    half_of = (expert_ids // per_half).astype(jnp.int32)

    def shard_step(total, shard):
        start = (shard * shard_width).astype(jnp.int32)
        act_piece = lax.dynamic_slice_in_dim(active_all, start, shard_width, 2).astype(jnp.float32)
        down_piece = lax.dynamic_slice_in_dim(w_down, start, shard_width, 1).astype(jnp.float32)
        slot_part = jnp.einsum('ecf,efd->ecd', act_piece, down_piece).reshape(EXPERTS * capacity, D)
        for half in range(N_EXPERT):
            part = jnp.zeros((seq_count, D), jnp.float32)
            for column in range(2):
                weight = jnp.where(half_of[:, column] == half, route_weights[:, column], 0.0)
                part = part + slot_part[flat_slot[:, column]] * weight[:, None]
            rounded = lax.optimization_barrier(part.astype(jnp.bfloat16))
            total = total + rounded.astype(jnp.float32)
        return (total, None)
    combined, _ = lax.scan(shard_step, jnp.zeros((seq_count, D), jnp.float32), jnp.arange(N_ATTN, dtype=jnp.int32))
    return (hidden, combined.astype(jnp.bfloat16))
```

```python
import functools
import math

import jax
import jax.numpy as jnp
from jax import lax
from jax.experimental import pallas as pl
from jax.experimental.pallas import tpu as pltpu
from jax.sharding import PartitionSpec as P

norm_eps = 1e-05


def plain_body(
    queries,
    keys,
    values,
    lengths,
    out_proj,
    residual,
    norm_gain,
    expert_ids,
    expert_slots,
    route_weights,
    w_gate,
    w_up,
    w_down,
):
    seq_local, head_local, head_dim = queries.shape
    kv_local = keys.shape[2]
    cache_len = keys.shape[1]
    groups = head_local // kv_local
    query_groups = queries.reshape(seq_local, kv_local, groups, head_dim)
    scores = jnp.einsum(
        "skgd,sjkd->skgj", query_groups, keys, preferred_element_type=jnp.float32
    ) / math.sqrt(head_dim)
    visible = lax.broadcasted_iota(jnp.int32, (seq_local, cache_len), 1) < lengths[:, None]
    scores = jnp.where(visible[:, None, None, :], scores, -jnp.inf)
    row_peak = jnp.max(scores, axis=-1, keepdims=True)
    expo = jnp.exp(scores - row_peak)
    attn_probs = (expo / jnp.sum(expo, axis=-1, keepdims=True)).astype(jnp.bfloat16)
    head_out = jnp.einsum("skgj,sjkd->skgd", attn_probs, values, preferred_element_type=jnp.float32)
    head_out = head_out.astype(jnp.bfloat16).reshape(seq_local, head_local * head_dim)
    half_mixed = jnp.dot(
        lax.all_gather(head_out, "attn", axis=0, tiled=True),
        out_proj,
        preferred_element_type=jnp.float32,
    )
    mixed = lax.psum(half_mixed.astype(jnp.bfloat16), "expert").astype(jnp.float32)
    hidden = (residual.astype(jnp.float32) + mixed).astype(jnp.bfloat16)
    hidden_f = hidden.astype(jnp.float32)
    model_width = norm_gain.shape[0]
    col_count = hidden.shape[1]
    square_sums = lax.psum(jnp.sum(hidden_f * hidden_f, axis=1), "attn")
    gain_part = lax.dynamic_slice_in_dim(norm_gain, lax.axis_index("attn") * col_count, col_count)
    outgoing = (
        hidden_f * lax.rsqrt(square_sums / model_width + norm_eps)[:, None] * gain_part[None, :]
    ).astype(jnp.bfloat16)
    gathered = lax.all_gather(outgoing, "attn", axis=1, tiled=True)
    seq_count = expert_ids.shape[0]
    capacity = 3 * seq_count // 4
    local_count = w_gate.shape[0]
    local_ids = expert_ids - lax.axis_index("expert") * local_count
    is_local = (local_ids >= 0) & (local_ids < local_count)
    flat_slot = jnp.where(is_local, local_ids * capacity + expert_slots, local_count * capacity)
    token_index = lax.broadcasted_iota(jnp.int32, (seq_count, 2), 0)
    slot_token = (
        jnp.full((local_count * capacity,), -1, jnp.int32)
        .at[flat_slot.reshape(-1)]
        .set(token_index.reshape(-1), mode="drop")
    )
    filled = slot_token >= 0
    packed = jnp.where(
        filled[:, None], gathered[jnp.maximum(slot_token, 0)], jnp.zeros((), jnp.bfloat16)
    )
    packed = packed.reshape(local_count, capacity, model_width)
    gate_act = jnp.einsum("ecd,edf->ecf", packed, w_gate, preferred_element_type=jnp.float32)
    up_act = jnp.einsum("ecd,edf->ecf", packed, w_up, preferred_element_type=jnp.float32)
    active = (jax.nn.silu(gate_act) * up_act).astype(jnp.bfloat16)
    slot_out = jnp.einsum("ecf,efd->ecd", active, w_down, preferred_element_type=jnp.float32)
    slot_out = slot_out.reshape(local_count * capacity, model_width)
    combined = jnp.zeros((seq_count, model_width), jnp.float32)
    for column in range(2):
        row_pick = jnp.minimum(flat_slot[:, column], local_count * capacity - 1)
        row_scale = jnp.where(is_local[:, column], route_weights[:, column], 0.0)
        combined = combined + slot_out[row_pick] * row_scale[:, None]
    rounded_part = lax.optimization_barrier(combined.astype(jnp.bfloat16)).astype(jnp.float32)
    feature_part = lax.psum_scatter(
        rounded_part.astype(jnp.bfloat16), "attn", scatter_dimension=1, tiled=True
    )
    row_total = lax.psum(feature_part, "expert").astype(jnp.float32)
    return (hidden, row_total.astype(jnp.bfloat16))


ROWS = 8
TILE = 256
MESH = pl.DeviceIdType.MESH


def near_first(count):
    return sorted(range(1, count), key=lambda k: (min(k, count - k), k))


def layer_kernel(
    n,
    kv,
    q_hbm,
    k_hbm,
    v_hbm,
    len_ref,
    wo_hbm,
    res_ref,
    gain_ref,
    ids_ref,
    rw_ref,
    wg_hbm,
    wu_hbm,
    wd_hbm,
    hid_out,
    exp_out,
    q_v,
    k_v,
    v_v,
    wo_v,
    wg_v,
    wu_v,
    wd_v,
    att,
    heads,
    mixed,
    mixed_in,
    xbuf,
    xs,
    acc_g,
    acc_u,
    act,
    pacc,
    core_out,
    core_in,
    y_out,
    y_in,
    z_out,
    z_in,
    last,
    in_sem,
    wo_sem,
    w_sem,
    d_sem,
    s1z,
    s1y,
    r1,
    sx,
    rx,
    s2z,
    s2y,
    s2c,
    r2,
    s3c,
    r3c,
    s3y,
    r3y,
    s3z,
    r3z,
    s4,
    r4,
):
    zs = n // 2
    chunks = heads.shape[1]
    head_count, head_dim = q_v.shape[1:]
    cache_rows = k_v.shape[1]
    cols = xbuf.shape[3]
    half_rows = xbuf.shape[2]
    rows = 2 * half_rows
    pair = 2 * cols
    width = n * cols
    ff = acc_g.shape[2]
    local_count = acc_g.shape[0]

    me = lax.axis_index("attn")
    core = lax.axis_index("expert")
    other = 1 - core
    z = me // 2
    y = me % 2
    partner = me + 1 - 2 * y

    def z_of(k):
        return lax.rem(z + k, zs)

    def z_from(k):
        return lax.rem(z + zs - k, zs)

    def at_attn(a):
        return {"attn": a}

    sibling = {"expert": other}

    def rcopy(src, dst, send, recv, dev):
        return pltpu.make_async_remote_copy(
            src_ref=src,
            dst_ref=dst,
            send_sem=send,
            recv_sem=recv,
            device_id=dev,
            device_id_type=MESH,
        )

    barrier = pltpu.get_barrier_semaphore()
    for k in range(1, zs):
        pl.semaphore_signal(barrier, inc=1, device_id=at_attn(2 * z_of(k) + y), device_id_type=MESH)
    pl.semaphore_signal(barrier, inc=1, device_id=at_attn(partner), device_id_type=MESH)
    pl.semaphore_signal(barrier, inc=1, device_id=sibling, device_id_type=MESH)

    def in_copies(c):
        rng = pl.ds(c * ROWS, ROWS)
        return [
            pltpu.make_async_copy(hbm.at[rng], vm.at[rng], in_sem.at[c, i])
            for i, (hbm, vm) in enumerate(((q_hbm, q_v), (k_hbm, k_v), (v_hbm, v_v)))
        ]

    for c in range(chunks):
        for copy in in_copies(c):
            copy.start()
    wo_copy = pltpu.make_async_copy(wo_hbm, wo_v, wo_sem)
    wo_copy.start()
    order = near_first(zs)

    def w_copies(k):
        rng = pl.ds(pl.multiple_of(z_of(zs - k) * pair, pair), pair)
        return [
            pltpu.make_async_copy(hbm.at[e, rng], vm.at[e, rng], w_sem.at[k, 2 * e + i])
            for e in range(local_count)
            for i, (hbm, vm) in enumerate(((wg_hbm, wg_v), (wu_hbm, wu_v)))
        ]

    for k in [0] + order:
        for copy in w_copies(k):
            copy.start()
    d_copies = [
        pltpu.make_async_copy(
            wd_hbm.at[e, :, pl.ds(b * pair, pair)],
            wd_v.at[b, pl.ds(e * ff, ff)],
            d_sem.at[b, e],
        )
        for b in range(zs)
        for e in range(local_count)
    ]
    for copy in d_copies:
        copy.start()

    col = lax.broadcasted_iota(jnp.int32, (head_count, cache_rows), 1)
    row = lax.broadcasted_iota(jnp.int32, (head_count, cache_rows), 0)
    col_pos = lax.shift_right_logical(col, kv.bit_length() - 1)
    col_kv = lax.bitwise_and(col, kv - 1)
    groups = head_count // kv
    same_kv = (row >= col_kv * groups) & (row < col_kv * groups + groups)
    live_pos = jnp.where(same_kv, col_pos, 1 << 20)

    def z_send(k, c):
        return rcopy(
            heads.at[me, c], heads.at[me, c], s1z.at[k, c], r1.at[me, c], at_attn(2 * z_of(k) + y)
        )

    def y_send(k, c):
        a = 2 * z_from(k) + y
        return rcopy(heads.at[a, c], heads.at[a, c], s1y.at[k, c], r1.at[a, c], at_attn(partner))

    def attend(c):
        for copy in in_copies(c):
            copy.wait()
        scores = []
        for i in range(ROWS):
            s = c * ROWS + i
            logits = lax.dot_general(
                q_v[s], k_v[s], (((1,), (1,)), ((), ())), preferred_element_type=jnp.float32
            )
            scores.append(jnp.where(live_pos < len_ref[s], logits, -1e30))
        scores = jnp.concatenate(scores, axis=0) * (1.0 / math.sqrt(head_dim))
        expo = jnp.exp(scores - jnp.max(scores, axis=-1, keepdims=True))
        probs = expo / jnp.sum(expo, axis=-1, keepdims=True)
        for i in range(ROWS):
            part = probs[i * head_count : (i + 1) * head_count].astype(jnp.bfloat16)
            att[pl.ds(i * head_count, head_count), :] = jnp.dot(
                part, v_v[c * ROWS + i], preferred_element_type=jnp.float32
            )
        for h in range(head_count):
            heads[me, c, :, h * head_dim : (h + 1) * head_dim] = att[
                pl.ds(h, ROWS, stride=head_count), :
            ].astype(jnp.bfloat16)

    for c in range(chunks):
        attend(c)
        if c == 0:
            pl.semaphore_wait(barrier, zs + 1)
        for k in order:
            z_send(k, c).start()
        y_send(0, c).start()

    for c in range(chunks):
        for k in order:
            y_send(k, c).wait_recv()
            y_send(k, c).start()
    for c in range(chunks):
        for k in [0] + order:
            a = 2 * z_from(k) + 1 - y
            rcopy(heads.at[a, c], heads.at[a, c], s1y.at[k, c], r1.at[a, c], at_attn(partner)).wait_recv()

    wo_copy.wait()
    proj = jnp.dot(
        heads[...].reshape(rows, head_count * head_dim), wo_v[...], preferred_element_type=jnp.float32
    )
    mixed[0] = proj[:half_rows]
    mixed[1] = proj[half_rows:]
    x_copy = rcopy(mixed.at[other], mixed_in, sx, rx, sibling)
    x_copy.start()
    x_copy.wait_recv()
    xbuf[me, core] = (res_ref[core].astype(jnp.float32) + mixed[core] + mixed_in[...]).astype(jnp.bfloat16)

    def x_z(k):
        return rcopy(
            xbuf.at[me, core], xbuf.at[me, core], s2z.at[k], r2.at[me, core], at_attn(2 * z_of(k) + y)
        )

    def x_y(k):
        a = 2 * z_from(k) + y
        return rcopy(xbuf.at[a, core], xbuf.at[a, core], s2y.at[k], r2.at[a, core], at_attn(partner))

    def x_c(a, half):
        return rcopy(xbuf.at[a, half], xbuf.at[a, half], s2c.at[a], r2.at[a, half], sibling)

    for k in order:
        x_z(k).start()
    x_y(0).start()
    x_c(me, core).start()

    def from_z(k):
        a = 2 * z_from(k) + y
        x_c(a, core).wait_recv()
        x_y(k).start()
        x_c(a, core).start()

    def from_y(k):
        a = 2 * z_from(k) + 1 - y
        x_c(a, core).wait_recv()
        x_c(a, core).start()

    def from_core(k):
        for side in range(2):
            x_c(2 * z_from(k) + side, other).wait_recv()

    def load_x(k, ssq):
        b = z_from(k)
        for side in range(2):
            block = xbuf[2 * b + side].reshape(rows, cols).astype(jnp.float32)
            ssq = ssq + jnp.sum(block * block, axis=1, keepdims=True)
            xs[:, side * cols : (side + 1) * cols] = (block * gain_ref[2 * b + side]).astype(jnp.bfloat16)
        return ssq

    def up_step(k, first):
        for copy in w_copies(k):
            copy.wait()
        rng = pl.ds(pl.multiple_of(z_from(k) * pair, pair), pair)
        for e in range(local_count):

            def tile(t, carry):
                at = pl.ds(pl.multiple_of(t * TILE, TILE), TILE)
                for acc, w in ((acc_g, wg_v), (acc_u, wu_v)):
                    part = jnp.dot(xs[...], w[e, rng, at], preferred_element_type=jnp.float32)
                    if first:
                        acc[e, :, at] = part
                    else:
                        acc[e, :, at] += part
                return carry

            lax.fori_loop(0, ff // TILE, tile, 0)

    near = order[:2]
    far = order[2:]
    from_y(0)
    for k in near:
        from_z(k)
    from_core(0)
    ssq = load_x(0, jnp.zeros((rows, 1), jnp.float32))
    up_step(0, True)
    for k in far:
        from_z(k)
    for k in order:
        from_y(k)
        from_core(k)
        ssq = load_x(k, ssq)
        up_step(k, False)
    for half in range(2):
        hid_out[half] = xbuf[me, half]

    row_scale = lax.rsqrt(ssq / width + norm_eps)
    for e in range(local_count):
        chosen = ids_ref[...] == core * local_count + e
        weight = jnp.sum(jnp.where(chosen, rw_ref[...], 0.0), axis=1, keepdims=True)
        weight = weight * row_scale

        def tile(t, carry):
            at = pl.ds(pl.multiple_of(t * TILE, TILE), TILE)
            gate = acc_g[e, :, at] * row_scale
            value = gate / (1.0 + jnp.exp(-gate)) * (acc_u[e, :, at] * weight)
            act[:, pl.ds(pl.multiple_of(e * ff + t * TILE, TILE), TILE)] = value.astype(jnp.bfloat16)
            return carry

        lax.fori_loop(0, ff // TILE, tile, 0)

    for copy in d_copies:
        copy.wait()

    def down(k):
        b = z_of(k)
        for t in range(0, pair, TILE):
            part = jnp.dot(act[...], wd_v[b, :, t : t + TILE], preferred_element_type=jnp.float32)
            for side in range(2):
                lo, hi = max(t, side * cols), min(t + TILE, (side + 1) * cols)
                if lo < hi:
                    for half in range(2):
                        pacc[k, side, half, :, lo - side * cols : hi - side * cols] = part[
                            half * half_rows : (half + 1) * half_rows, lo - t : hi - t
                        ]
        core_out[k] = pacc[k, :, other].astype(jnp.bfloat16)
        core_copy(k).start()

    def core_copy(k):
        return rcopy(core_out.at[k], core_in.at[k], s3c.at[k], r3c.at[k], sibling)

    def y_copy(k):
        return rcopy(y_out.at[k], y_in.at[k], s3y.at[k], r3y.at[k], at_attn(partner))

    def z_copy(k):
        return rcopy(z_out.at[k], z_in.at[k], s3z.at[k], r3z.at[k], at_attn(2 * z_of(k) + y))

    def core_sum(k):
        core_copy(k).wait_recv()
        y_out[k] = (pacc[k, 1 - y, core] + core_in[k, 1 - y].astype(jnp.float32)).astype(jnp.bfloat16)
        y_copy(k).start()

    def y_sum(k):
        y_copy(k).wait_recv()
        total = (
            pacc[k, y, core] + core_in[k, y].astype(jnp.float32) + y_in[k].astype(jnp.float32)
        )
        if k == 0:
            return total
        z_out[k] = total.astype(jnp.bfloat16)
        z_copy(k).start()

    steps = order[::-1] + [0]
    for i in range(len(steps) + 2):
        if i < len(steps):
            down(steps[i])
        if 1 <= i <= len(steps):
            core_sum(steps[i - 1])
        if i >= 2:
            total = y_sum(steps[i - 2])
    for k in steps[:-1]:
        z_copy(k).wait_recv()
        total = total + z_in[k].astype(jnp.float32)
    last[core] = total.astype(jnp.bfloat16)
    last_copy = rcopy(last.at[core], last.at[core], s4, r4, sibling)
    last_copy.start()

    x_copy.wait_send()
    for c in range(chunks):
        for k in order:
            z_send(k, c).wait_send()
        for k in range(zs):
            y_send(k, c).wait_send()
    for k in order:
        x_z(k).wait_send()
    for k in range(zs):
        x_y(k).wait_send()
        core_copy(k).wait_send()
        y_copy(k).wait_send()
        if k:
            z_copy(k).wait_send()
    for a in range(n):
        x_c(a, core).wait_send()
    last_copy.wait_send()
    rcopy(last.at[other], last.at[other], s4, r4, sibling).wait_recv()
    exp_out[...] = last[...]


def body(n, *operands):
    (queries, keys, values, lengths, out_proj, residual, norm_gain) = operands[:7]
    (expert_ids, expert_slots, route_weights, w_gate, w_up, w_down) = operands[7:]
    seqs, head_count, head_dim = queries.shape
    cache_len, kv = keys.shape[1:3]
    rows, cols = residual.shape
    local_count, width, ff = w_gate.shape
    fits = (
        n % 2 == 0
        and seqs % ROWS == 0
        and kv & (kv - 1) == 0
        and cols % 128 == 0
        and (2 * cols) % TILE == 0
        and ff % TILE == 0
        and rows % 32 == 0
    )
    if not fits:
        return plain_body(*operands)
    zs, chunks, half = n // 2, seqs // ROWS, rows // 2
    bf16, f32 = jnp.bfloat16, jnp.float32
    dma = pltpu.SemaphoreType.DMA
    vmem = pl.BlockSpec(memory_space=pltpu.VMEM)
    hbm = pl.BlockSpec(memory_space=pl.ANY)
    hidden, out = pl.pallas_call(
        functools.partial(layer_kernel, n, kv),
        out_shape=[jax.ShapeDtypeStruct((2, half, cols), bf16)] * 2,
        in_specs=[hbm, hbm, hbm, pl.BlockSpec(memory_space=pltpu.SMEM), hbm, vmem, vmem, vmem, vmem]
        + [hbm] * 3,
        out_specs=[vmem, vmem],
        scratch_shapes=[
            pltpu.VMEM((seqs, head_count, head_dim), bf16),
            pltpu.VMEM((seqs, cache_len * kv, head_dim), bf16),
            pltpu.VMEM((seqs, cache_len * kv, head_dim), bf16),
            pltpu.VMEM(out_proj.shape, bf16),
            pltpu.VMEM(w_gate.shape, bf16),
            pltpu.VMEM(w_up.shape, bf16),
            pltpu.VMEM((zs, local_count * ff, 2 * cols), bf16),
            pltpu.VMEM((ROWS * head_count, head_dim), f32),
            pltpu.VMEM((n, chunks, ROWS, head_count * head_dim), bf16),
            pltpu.VMEM((2, half, cols), f32),
            pltpu.VMEM((half, cols), f32),
            pltpu.VMEM((n, 2, half, cols), bf16),
            pltpu.VMEM((rows, 2 * cols), bf16),
            pltpu.VMEM((local_count, rows, ff), f32),
            pltpu.VMEM((local_count, rows, ff), f32),
            pltpu.VMEM((rows, local_count * ff), bf16),
            pltpu.VMEM((zs, 2, 2, half, cols), f32),
            pltpu.VMEM((zs, 2, half, cols), bf16),
            pltpu.VMEM((zs, 2, half, cols), bf16),
            pltpu.VMEM((zs, half, cols), bf16),
            pltpu.VMEM((zs, half, cols), bf16),
            pltpu.VMEM((zs, half, cols), bf16),
            pltpu.VMEM((zs, half, cols), bf16),
            pltpu.VMEM((2, half, cols), bf16),
            dma((chunks, 3)),
            dma,
            dma((zs, 2 * local_count)),
            dma((zs, local_count)),
            dma((zs, chunks)),
            dma((zs, chunks)),
            dma((n, chunks)),
            dma,
            dma,
            dma((zs,)),
            dma((zs,)),
            dma((n,)),
            dma((n, 2)),
            dma((zs,)),
            dma((zs,)),
            dma((zs,)),
            dma((zs,)),
            dma((zs,)),
            dma((zs,)),
            dma,
            dma,
        ],
        compiler_params=pltpu.CompilerParams(
            collective_id=0, has_side_effects=True, vmem_limit_bytes=62 * 1024 * 1024
        ),
    )(
        queries,
        keys.reshape(seqs, cache_len * kv, head_dim),
        values.reshape(seqs, cache_len * kv, head_dim),
        lengths,
        out_proj,
        residual.reshape(2, half, cols),
        norm_gain.reshape(n, 1, cols),
        expert_ids,
        route_weights,
        w_gate,
        w_up,
        w_down,
    )
    return hidden.reshape(rows, cols), out.reshape(rows, cols)


def solution(mesh):
    return jax.shard_map(
        functools.partial(body, mesh.shape["attn"]),
        mesh=mesh,
        in_specs=(
            P(("group", "attn"), "expert", None),
            P(("group", "attn"), None, "expert", None),
            P(("group", "attn"), None, "expert", None),
            P(("group", "attn")),
            P("expert", "attn"),
            P("group", "attn"),
            P(),
            P("group", None),
            P("group", None),
            P("group", None),
            P("expert", None, "attn"),
            P("expert", None, "attn"),
            P("expert", "attn", None),
        ),
        out_specs=(P("group", "attn"), P("group", "attn")),
        check_vma=False,
    )
```

```python
import functools
import math

import jax
import jax.numpy as jnp
from jax import lax
from jax.experimental import pallas as pl
from jax.experimental.pallas import tpu as pltpu
from jax.sharding import PartitionSpec as P

norm_eps = 1e-05


def plain_body(
    queries,
    keys,
    values,
    lengths,
    out_proj,
    residual,
    norm_gain,
    expert_ids,
    expert_slots,
    route_weights,
    w_gate,
    w_up,
    w_down,
):
    seq_local, head_local, head_dim = queries.shape
    kv_local = keys.shape[2]
    cache_len = keys.shape[1]
    groups = head_local // kv_local
    query_groups = queries.reshape(seq_local, kv_local, groups, head_dim)
    scores = jnp.einsum(
        "skgd,sjkd->skgj", query_groups, keys, preferred_element_type=jnp.float32
    ) / math.sqrt(head_dim)
    visible = lax.broadcasted_iota(jnp.int32, (seq_local, cache_len), 1) < lengths[:, None]
    scores = jnp.where(visible[:, None, None, :], scores, -jnp.inf)
    row_peak = jnp.max(scores, axis=-1, keepdims=True)
    expo = jnp.exp(scores - row_peak)
    attn_probs = (expo / jnp.sum(expo, axis=-1, keepdims=True)).astype(jnp.bfloat16)
    head_out = jnp.einsum("skgj,sjkd->skgd", attn_probs, values, preferred_element_type=jnp.float32)
    head_out = head_out.astype(jnp.bfloat16).reshape(seq_local, head_local * head_dim)
    half_mixed = jnp.dot(
        lax.all_gather(head_out, "attn", axis=0, tiled=True),
        out_proj,
        preferred_element_type=jnp.float32,
    )
    mixed = lax.psum(half_mixed.astype(jnp.bfloat16), "expert").astype(jnp.float32)
    hidden = (residual.astype(jnp.float32) + mixed).astype(jnp.bfloat16)
    hidden_f = hidden.astype(jnp.float32)
    model_width = norm_gain.shape[0]
    col_count = hidden.shape[1]
    square_sums = lax.psum(jnp.sum(hidden_f * hidden_f, axis=1), "attn")
    gain_part = lax.dynamic_slice_in_dim(norm_gain, lax.axis_index("attn") * col_count, col_count)
    outgoing = (
        hidden_f * lax.rsqrt(square_sums / model_width + norm_eps)[:, None] * gain_part[None, :]
    ).astype(jnp.bfloat16)
    gathered = lax.all_gather(outgoing, "attn", axis=1, tiled=True)
    seq_count = expert_ids.shape[0]
    capacity = 3 * seq_count // 4
    local_count = w_gate.shape[0]
    local_ids = expert_ids - lax.axis_index("expert") * local_count
    is_local = (local_ids >= 0) & (local_ids < local_count)
    flat_slot = jnp.where(is_local, local_ids * capacity + expert_slots, local_count * capacity)
    token_index = lax.broadcasted_iota(jnp.int32, (seq_count, 2), 0)
    slot_token = (
        jnp.full((local_count * capacity,), -1, jnp.int32)
        .at[flat_slot.reshape(-1)]
        .set(token_index.reshape(-1), mode="drop")
    )
    filled = slot_token >= 0
    packed = jnp.where(
        filled[:, None], gathered[jnp.maximum(slot_token, 0)], jnp.zeros((), jnp.bfloat16)
    )
    packed = packed.reshape(local_count, capacity, model_width)
    gate_act = jnp.einsum("ecd,edf->ecf", packed, w_gate, preferred_element_type=jnp.float32)
    up_act = jnp.einsum("ecd,edf->ecf", packed, w_up, preferred_element_type=jnp.float32)
    active = (jax.nn.silu(gate_act) * up_act).astype(jnp.bfloat16)
    slot_out = jnp.einsum("ecf,efd->ecd", active, w_down, preferred_element_type=jnp.float32)
    slot_out = slot_out.reshape(local_count * capacity, model_width)
    combined = jnp.zeros((seq_count, model_width), jnp.float32)
    for column in range(2):
        row_pick = jnp.minimum(flat_slot[:, column], local_count * capacity - 1)
        row_scale = jnp.where(is_local[:, column], route_weights[:, column], 0.0)
        combined = combined + slot_out[row_pick] * row_scale[:, None]
    rounded_part = lax.optimization_barrier(combined.astype(jnp.bfloat16)).astype(jnp.float32)
    feature_part = lax.psum_scatter(
        rounded_part.astype(jnp.bfloat16), "attn", scatter_dimension=1, tiled=True
    )
    row_total = lax.psum(feature_part, "expert").astype(jnp.float32)
    return (hidden, row_total.astype(jnp.bfloat16))


ROWS = 8
TILE = 256
MESH = pl.DeviceIdType.MESH


def near_first(count):
    return sorted(range(1, count), key=lambda k: (min(k, count - k), k))


def layer_kernel(
    n,
    kv,
    q_hbm,
    k_hbm,
    v_hbm,
    len_ref,
    wo_hbm,
    res_ref,
    gain_ref,
    ids_ref,
    rw_ref,
    wg_hbm,
    wu_hbm,
    wd_hbm,
    hid_out,
    exp_out,
    q_v,
    k_v,
    v_v,
    wo_v,
    wg_v,
    wu_v,
    wd_v,
    att,
    heads,
    mixed,
    mixed_in,
    xbuf,
    xs,
    acc_g,
    acc_u,
    act,
    pacc,
    core_out,
    core_in,
    y_out,
    y_in,
    z_out,
    z_in,
    last,
    in_sem,
    wo_sem,
    w_sem,
    d_sem,
    s1z,
    s1y,
    r1,
    sx,
    rx,
    s2z,
    s2y,
    s2c,
    r2,
    s3c,
    r3c,
    s3y,
    r3y,
    s3z,
    r3z,
    s4,
    r4,
):
    zs = n // 2
    chunks = heads.shape[1]
    head_count, head_dim = q_v.shape[1:]
    cache_rows = k_v.shape[1]
    cols = xbuf.shape[3]
    half_rows = xbuf.shape[2]
    rows = 2 * half_rows
    pair = 2 * cols
    width = n * cols
    ff = acc_g.shape[2]
    local_count = acc_g.shape[0]

    me = lax.axis_index("attn")
    core = lax.axis_index("expert")
    other = 1 - core
    z = me // 2
    y = me % 2
    partner = me + 1 - 2 * y

    def z_of(k):
        return lax.rem(z + k, zs)

    def z_from(k):
        return lax.rem(z + zs - k, zs)

    def at_attn(a):
        return {"attn": a}

    sibling = {"expert": other}

    def rcopy(src, dst, send, recv, dev):
        return pltpu.make_async_remote_copy(
            src_ref=src,
            dst_ref=dst,
            send_sem=send,
            recv_sem=recv,
            device_id=dev,
            device_id_type=MESH,
        )

    barrier = pltpu.get_barrier_semaphore()
    for k in range(1, zs):
        pl.semaphore_signal(barrier, inc=1, device_id=at_attn(2 * z_of(k) + y), device_id_type=MESH)
    pl.semaphore_signal(barrier, inc=1, device_id=at_attn(partner), device_id_type=MESH)
    pl.semaphore_signal(barrier, inc=1, device_id=sibling, device_id_type=MESH)

    def in_copies(c):
        rng = pl.ds(c * ROWS, ROWS)
        return [
            pltpu.make_async_copy(hbm.at[rng], vm.at[rng], in_sem.at[c, i])
            for i, (hbm, vm) in enumerate(((q_hbm, q_v), (k_hbm, k_v), (v_hbm, v_v)))
        ]

    for c in range(chunks):
        for copy in in_copies(c):
            copy.start()
    wo_copy = pltpu.make_async_copy(wo_hbm, wo_v, wo_sem)
    wo_copy.start()
    order = near_first(zs)

    def w_copies(k):
        rng = pl.ds(pl.multiple_of(z_of(zs - k) * pair, pair), pair)
        return [
            pltpu.make_async_copy(hbm.at[e, rng], vm.at[e, rng], w_sem.at[k, 2 * e + i])
            for e in range(local_count)
            for i, (hbm, vm) in enumerate(((wg_hbm, wg_v), (wu_hbm, wu_v)))
        ]

    for k in [0] + order:
        for copy in w_copies(k):
            copy.start()
    d_copies = [
        pltpu.make_async_copy(
            wd_hbm.at[e, :, pl.ds(b * pair, pair)],
            wd_v.at[b, pl.ds(e * ff, ff)],
            d_sem.at[b, e],
        )
        for b in range(zs)
        for e in range(local_count)
    ]
    for copy in d_copies:
        copy.start()

    col = lax.broadcasted_iota(jnp.int32, (head_count, cache_rows), 1)
    row = lax.broadcasted_iota(jnp.int32, (head_count, cache_rows), 0)
    col_pos = lax.shift_right_logical(col, kv.bit_length() - 1)
    col_kv = lax.bitwise_and(col, kv - 1)
    groups = head_count // kv
    same_kv = (row >= col_kv * groups) & (row < col_kv * groups + groups)
    live_pos = jnp.where(same_kv, col_pos, 1 << 20)

    def z_send(k, c):
        return rcopy(
            heads.at[me, c], heads.at[me, c], s1z.at[k, c], r1.at[me, c], at_attn(2 * z_of(k) + y)
        )

    def y_send(k, c):
        a = 2 * z_from(k) + y
        return rcopy(heads.at[a, c], heads.at[a, c], s1y.at[k, c], r1.at[a, c], at_attn(partner))

    def attend(c):
        for copy in in_copies(c):
            copy.wait()
        scores = []
        for i in range(ROWS):
            s = c * ROWS + i
            logits = lax.dot_general(
                q_v[s], k_v[s], (((1,), (1,)), ((), ())), preferred_element_type=jnp.float32
            )
            scores.append(jnp.where(live_pos < len_ref[s], logits, -1e30))
        scores = jnp.concatenate(scores, axis=0) * (1.0 / math.sqrt(head_dim))
        expo = jnp.exp(scores - jnp.max(scores, axis=-1, keepdims=True))
        probs = expo / jnp.sum(expo, axis=-1, keepdims=True)
        for i in range(ROWS):
            part = probs[i * head_count : (i + 1) * head_count].astype(jnp.bfloat16)
            att[pl.ds(i * head_count, head_count), :] = jnp.dot(
                part, v_v[c * ROWS + i], preferred_element_type=jnp.float32
            )
        for h in range(head_count):
            heads[me, c, :, h * head_dim : (h + 1) * head_dim] = att[
                pl.ds(h, ROWS, stride=head_count), :
            ].astype(jnp.bfloat16)

    for c in range(chunks):
        attend(c)
        if c == 0:
            pl.semaphore_wait(barrier, zs + 1)
        for k in order:
            z_send(k, c).start()
        y_send(0, c).start()

    for c in range(chunks):
        for k in order:
            y_send(k, c).wait_recv()
            y_send(k, c).start()
    for c in range(chunks):
        for k in [0] + order:
            a = 2 * z_from(k) + 1 - y
            rcopy(heads.at[a, c], heads.at[a, c], s1y.at[k, c], r1.at[a, c], at_attn(partner)).wait_recv()

    wo_copy.wait()
    proj = jnp.dot(
        heads[...].reshape(rows, head_count * head_dim), wo_v[...], preferred_element_type=jnp.float32
    )
    mixed[0] = proj[:half_rows]
    mixed[1] = proj[half_rows:]
    x_copy = rcopy(mixed.at[other], mixed_in, sx, rx, sibling)
    x_copy.start()
    x_copy.wait_recv()
    xbuf[me, core] = (res_ref[core].astype(jnp.float32) + mixed[core] + mixed_in[...]).astype(jnp.bfloat16)

    def x_z(k):
        return rcopy(
            xbuf.at[me, core], xbuf.at[me, core], s2z.at[k], r2.at[me, core], at_attn(2 * z_of(k) + y)
        )

    def x_y(k):
        a = 2 * z_from(k) + y
        return rcopy(xbuf.at[a, core], xbuf.at[a, core], s2y.at[k], r2.at[a, core], at_attn(partner))

    def x_c(a, half):
        return rcopy(xbuf.at[a, half], xbuf.at[a, half], s2c.at[a], r2.at[a, half], sibling)

    for k in order:
        x_z(k).start()
    x_y(0).start()
    x_c(me, core).start()

    def from_z(k):
        a = 2 * z_from(k) + y
        x_c(a, core).wait_recv()
        x_y(k).start()
        x_c(a, core).start()

    def from_y(k):
        a = 2 * z_from(k) + 1 - y
        x_c(a, core).wait_recv()
        x_c(a, core).start()

    def from_core(k):
        for side in range(2):
            x_c(2 * z_from(k) + side, other).wait_recv()

    def load_x(k, ssq):
        b = z_from(k)
        for side in range(2):
            block = xbuf[2 * b + side].reshape(rows, cols).astype(jnp.float32)
            ssq = ssq + jnp.sum(block * block, axis=1, keepdims=True)
            xs[:, side * cols : (side + 1) * cols] = (block * gain_ref[2 * b + side]).astype(jnp.bfloat16)
        return ssq

    def up_step(k, first, experts):
        if 0 in experts:
            for copy in w_copies(k):
                copy.wait()
        rng = pl.ds(pl.multiple_of(z_from(k) * pair, pair), pair)
        for e in experts:

            def tile(t, carry):
                at = pl.ds(pl.multiple_of(t * TILE, TILE), TILE)
                for acc, w in ((acc_g, wg_v), (acc_u, wu_v)):
                    part = jnp.dot(xs[...], w[e, rng, at], preferred_element_type=jnp.float32)
                    if first:
                        acc[e, :, at] = part
                    else:
                        acc[e, :, at] += part
                return carry

            lax.fori_loop(0, ff // TILE, tile, 0)

    near = order[:2]
    far = order[2:]
    from_y(0)
    for k in near:
        from_z(k)
    from_core(0)
    ssq = load_x(0, jnp.zeros((rows, 1), jnp.float32))
    up_step(0, True, range(1))
    for k in far:
        from_z(k)
    up_step(0, True, range(1, local_count))
    for k in near:
        from_y(k)
    for i, k in enumerate(order):
        from_core(k)
        ssq = load_x(k, ssq)
        up_step(k, False, range(1))
        if i == 0:
            for j in far:
                from_y(j)
        up_step(k, False, range(1, local_count))
    for half in range(2):
        hid_out[half] = xbuf[me, half]

    row_scale = lax.rsqrt(ssq / width + norm_eps)
    diagonal = lax.broadcasted_iota(jnp.int32, (rows, rows), 0) == lax.broadcasted_iota(
        jnp.int32, (rows, rows), 1
    )
    for e in range(local_count):
        chosen = ids_ref[...] == core * local_count + e
        token_weight = jnp.sum(jnp.where(chosen, rw_ref[...], 0.0), axis=0, keepdims=True)
        weight = jnp.sum(jnp.where(diagonal, token_weight, 0.0), axis=1, keepdims=True)
        weight = weight * row_scale

        def tile(t, carry):
            at = pl.ds(pl.multiple_of(t * TILE, TILE), TILE)
            gate = acc_g[e, :, at] * row_scale
            value = gate / (1.0 + jnp.exp(-gate)) * (acc_u[e, :, at] * weight)
            act[:, pl.ds(pl.multiple_of(e * ff + t * TILE, TILE), TILE)] = value.astype(jnp.bfloat16)
            return carry

        lax.fori_loop(0, ff // TILE, tile, 0)

    for copy in d_copies:
        copy.wait()

    def down(k):
        b = z_of(k)
        for t in range(0, pair, TILE):
            part = jnp.dot(act[...], wd_v[b, :, t : t + TILE], preferred_element_type=jnp.float32)
            for side in range(2):
                lo, hi = max(t, side * cols), min(t + TILE, (side + 1) * cols)
                if lo < hi:
                    for half in range(2):
                        pacc[k, side, half, :, lo - side * cols : hi - side * cols] = part[
                            half * half_rows : (half + 1) * half_rows, lo - t : hi - t
                        ]
        core_out[k] = pacc[k, :, other].astype(jnp.bfloat16)
        core_copy(k).start()

    def core_copy(k):
        return rcopy(core_out.at[k], core_in.at[k], s3c.at[k], r3c.at[k], sibling)

    def y_copy(k):
        return rcopy(y_out.at[k], y_in.at[k], s3y.at[k], r3y.at[k], at_attn(partner))

    def z_copy(k):
        return rcopy(z_out.at[k], z_in.at[k], s3z.at[k], r3z.at[k], at_attn(2 * z_of(k) + y))

    def core_sum(k):
        core_copy(k).wait_recv()
        y_out[k] = (pacc[k, 1 - y, core] + core_in[k, 1 - y].astype(jnp.float32)).astype(jnp.bfloat16)
        y_copy(k).start()

    def y_sum(k):
        y_copy(k).wait_recv()
        total = (
            pacc[k, y, core] + core_in[k, y].astype(jnp.float32) + y_in[k].astype(jnp.float32)
        )
        if k == 0:
            return total
        z_out[k] = total.astype(jnp.bfloat16)
        z_copy(k).start()

    steps = order[::-1] + [0]
    for i in range(len(steps) + 2):
        if i < len(steps):
            down(steps[i])
        if 1 <= i <= len(steps):
            core_sum(steps[i - 1])
        if i >= 2:
            total = y_sum(steps[i - 2])
    for k in steps[:-1]:
        z_copy(k).wait_recv()
        total = total + z_in[k].astype(jnp.float32)
    last[core] = total.astype(jnp.bfloat16)
    last_copy = rcopy(last.at[core], last.at[core], s4, r4, sibling)
    last_copy.start()

    x_copy.wait_send()
    for c in range(chunks):
        for k in order:
            z_send(k, c).wait_send()
        for k in range(zs):
            y_send(k, c).wait_send()
    for k in order:
        x_z(k).wait_send()
    for k in range(zs):
        x_y(k).wait_send()
        core_copy(k).wait_send()
        y_copy(k).wait_send()
        if k:
            z_copy(k).wait_send()
    for a in range(n):
        x_c(a, core).wait_send()
    last_copy.wait_send()
    rcopy(last.at[other], last.at[other], s4, r4, sibling).wait_recv()
    exp_out[...] = last[...]


def write_kernel(hidden, expert, hidden_out, expert_out, sem):
    copies = [
        pltpu.make_async_copy(hidden, hidden_out, sem.at[0]),
        pltpu.make_async_copy(expert, expert_out, sem.at[1]),
    ]
    for copy in copies:
        copy.start()
    for copy in copies:
        copy.wait()


def body(n, *operands):
    (queries, keys, values, lengths, out_proj, residual, norm_gain) = operands[:7]
    (expert_ids, expert_slots, route_weights, w_gate, w_up, w_down) = operands[7:]
    seqs, head_count, head_dim = queries.shape
    cache_len, kv = keys.shape[1:3]
    rows, cols = residual.shape
    local_count, width, ff = w_gate.shape
    fits = (
        n % 2 == 0
        and seqs % ROWS == 0
        and kv & (kv - 1) == 0
        and cols % 128 == 0
        and (2 * cols) % TILE == 0
        and ff % TILE == 0
        and rows % 32 == 0
    )
    if not fits:
        return plain_body(*operands)
    zs, chunks, half = n // 2, seqs // ROWS, rows // 2
    bf16, f32 = jnp.bfloat16, jnp.float32
    dma = pltpu.SemaphoreType.DMA
    vmem = pl.BlockSpec(memory_space=pltpu.VMEM)
    hbm = pl.BlockSpec(memory_space=pl.ANY)
    hidden, out = pl.pallas_call(
        functools.partial(layer_kernel, n, kv),
        out_shape=[jax.ShapeDtypeStruct((2, half, cols), bf16)] * 2,
        in_specs=[hbm, hbm, hbm, pl.BlockSpec(memory_space=pltpu.SMEM), hbm, vmem, vmem, vmem, vmem]
        + [hbm] * 3,
        out_specs=[vmem, vmem],
        scratch_shapes=[
            pltpu.VMEM((seqs, head_count, head_dim), bf16),
            pltpu.VMEM((seqs, cache_len * kv, head_dim), bf16),
            pltpu.VMEM((seqs, cache_len * kv, head_dim), bf16),
            pltpu.VMEM(out_proj.shape, bf16),
            pltpu.VMEM(w_gate.shape, bf16),
            pltpu.VMEM(w_up.shape, bf16),
            pltpu.VMEM((zs, local_count * ff, 2 * cols), bf16),
            pltpu.VMEM((ROWS * head_count, head_dim), f32),
            pltpu.VMEM((n, chunks, ROWS, head_count * head_dim), bf16),
            pltpu.VMEM((2, half, cols), f32),
            pltpu.VMEM((half, cols), f32),
            pltpu.VMEM((n, 2, half, cols), bf16),
            pltpu.VMEM((rows, 2 * cols), bf16),
            pltpu.VMEM((local_count, rows, ff), f32),
            pltpu.VMEM((local_count, rows, ff), f32),
            pltpu.VMEM((rows, local_count * ff), bf16),
            pltpu.VMEM((zs, 2, 2, half, cols), f32),
            pltpu.VMEM((zs, 2, half, cols), bf16),
            pltpu.VMEM((zs, 2, half, cols), bf16),
            pltpu.VMEM((zs, half, cols), bf16),
            pltpu.VMEM((zs, half, cols), bf16),
            pltpu.VMEM((zs, half, cols), bf16),
            pltpu.VMEM((zs, half, cols), bf16),
            pltpu.VMEM((2, half, cols), bf16),
            dma((chunks, 3)),
            dma,
            dma((zs, 2 * local_count)),
            dma((zs, local_count)),
            dma((zs, chunks)),
            dma((zs, chunks)),
            dma((n, chunks)),
            dma,
            dma,
            dma((zs,)),
            dma((zs,)),
            dma((n,)),
            dma((n, 2)),
            dma((zs,)),
            dma((zs,)),
            dma((zs,)),
            dma((zs,)),
            dma((zs,)),
            dma((zs,)),
            dma,
            dma,
        ],
        compiler_params=pltpu.CompilerParams(
            collective_id=0, has_side_effects=True, vmem_limit_bytes=62 * 1024 * 1024
        ),
    )(
        queries,
        keys.reshape(seqs, cache_len * kv, head_dim),
        values.reshape(seqs, cache_len * kv, head_dim),
        lengths,
        out_proj,
        residual.reshape(2, half, cols),
        norm_gain.reshape(n, 1, cols),
        expert_ids.T,
        route_weights.T,
        w_gate,
        w_up,
        w_down,
    )
    return hidden.reshape(rows, cols), out.reshape(rows, cols)


def solution(mesh):
    return jax.shard_map(
        functools.partial(body, mesh.shape["attn"]),
        mesh=mesh,
        in_specs=(
            P(("group", "attn"), "expert", None),
            P(("group", "attn"), None, "expert", None),
            P(("group", "attn"), None, "expert", None),
            P(("group", "attn")),
            P("expert", "attn"),
            P("group", "attn"),
            P(),
            P("group", None),
            P("group", None),
            P("group", None),
            P("expert", None, "attn"),
            P("expert", None, "attn"),
            P("expert", "attn", None),
        ),
        out_specs=(P("group", "attn"), P("group", "attn")),
        check_vma=False,
    )
```
